32 devices in a mesh: series: 8 (over z, y), tm: 4 (over x, core).
Axes of the slice: x: 2, y: 2, z: 4, core: 2. Of those that a mesh axis runs over, the one named last changes fastest.
Arguments:
- target: float32 [8, 16384], P('tm', 'series'), may hold values from -14 to 14
- location: float32 [8, 16384], P('tm', 'series'), may hold values from -6 to 6
- variance: float32 [8, 16384], P('tm', 'series'), may hold values from 0.25 to 4
- factor_drift: bfloat16 [8, 64, 16384], P('tm', None, 'series'), may hold values from -0.0234375 to 0.0234375
- loading: bfloat16 [64, 16384], P(None, ('series', 'tm'))
- node_ids: int32 [3, 16384], P(None, 'series'), may hold values from 0 to 2047, as said below
- level_weight: float32 [4, 8], P(None, 'tm'), may hold values from 0.5 to 2
Outputs:
- gradient_location: float32 [8, 16384], P('tm', 'series')
- gradient_variance: float32 [8, 16384], P('tm', 'series')
- gradient_drift: float32 [8, 64, 16384], P('tm', None, 'series')
- gradient_loading: float32 [64, 16384], P(None, ('series', 'tm'))
The draws below stay inside these ranges and needn't reach their ends.
Inputs may be any that keep to these rules, and one draw needn't show every extreme that they name: `node_ids`: at each upper level node numbers never fall along the series, begin at 0 and rise by at most one from a series to the next; every node of a level is a union of whole nodes of the level below; a level-one node holds 5 series or more; every level-two node but the last holds 64 level-one nodes or more (one at least), every level-three node but the last 4 level-two nodes or more; level one has exactly 2048 nodes.
All inputs are finite; a program needn't handle non-finite values.
Results may differ from the reference program's by a relative error of at most 0.0003.
Values may be sent and summed in bfloat16 or wider, within the bound.
A program may use at most 64 MiB of HBM per device.

```python
import math
import jax
import jax.numpy as jnp
from jax import lax

R = 64
LEVELS = 4
SER_DEV = 2048
STEPS = 8
SERIES = 16384


def hierarchy_nodes(key):
    positions = jnp.arange(SERIES, dtype=jnp.int32)
    span_count = SERIES // 4 + 2
    first_key, second_key, third_key = jax.random.split(key, 3)
    block_count = SERIES // 8
    offsets = jax.random.randint(first_key, (block_count,), 0, 4).astype(jnp.int32)
    offsets = jnp.where(jnp.arange(block_count, dtype=jnp.int32) == 0, 0, offsets).astype(jnp.int32)
    block_index = positions // 8
    inside = positions % 8
    level_one = (block_index - (inside < jnp.take(offsets, block_index, axis=0)).astype(jnp.int32)).astype(jnp.int32)
    group_size = SER_DEV // 16
    lengths_two = jax.random.randint(second_key, (span_count,), max(group_size // 2, 1), group_size + group_size // 2 + 1)
    level_two = jnp.searchsorted(jnp.cumsum(lengths_two), level_one, side='right').astype(jnp.int32)
    lengths_three = jax.random.randint(third_key, (span_count,), 4, 13)
    level_three = jnp.searchsorted(jnp.cumsum(lengths_three), level_two, side='right').astype(jnp.int32)
    return jnp.stack([level_one, level_two, level_three])


def draw_node_ids(key, part):
    nodes = hierarchy_nodes(key)
    return nodes


def draw_loading(key, part):
    nodes = hierarchy_nodes(key)
    key = jax.random.fold_in(key, 23)
    subkeys = jax.random.split(key, 4)
    common = 0.35
    values = 0.5 * jnp.clip(jax.random.normal(subkeys[0], (R, SERIES), jnp.float32), -4.0, 4.0)
    for level_index in range(3):
        node_table = jnp.clip(jax.random.normal(subkeys[level_index + 1], (R, SERIES // 4 + 1), jnp.float32), -4.0, 4.0)
        values = values + common * jnp.take(node_table, nodes[level_index], axis=1)
    return (values * SERIES ** (-0.5)).astype(jnp.bfloat16)


def draw_target(key, part):
    nodes = hierarchy_nodes(key)
    key = jax.random.fold_in(key, 37)
    subkeys = jax.random.split(key, 4)
    values = jnp.clip(jax.random.normal(subkeys[0], (STEPS, SERIES), jnp.float32), -6.0, 6.0)
    amplitude = (1.0, 0.4, 0.3)
    for level_index in range(3):
        node_table = jnp.clip(jax.random.normal(subkeys[level_index + 1], (STEPS, SERIES // 4 + 1), jnp.float32), -4.0, 4.0)
        values = values + amplitude[level_index] * jnp.take(node_table, nodes[level_index], axis=1)
    return values


def steps_of(key, shape, pieces, smallest, largest):
    def one(dim, shards_of):
        draws = jax.random.uniform(jax.random.fold_in(jax.random.fold_in(key, 6), dim), (shards_of,), jnp.float32, smallest / len(pieces), largest / len(pieces))
        return jnp.repeat(jnp.exp(draws), shape[dim] // shards_of).reshape((-1,) + (1,) * (len(shape) - dim - 1))

    factor_of = one(*pieces[0])
    for cut in pieces[1:]:
        factor_of = factor_of * one(*cut)
    return factor_of


def bell_draw(own_key, extent, scale, limit, pieces=(), kind=jnp.bfloat16):
    factor_of = steps_of(own_key, extent, pieces, -0.22, 0.18) if pieces else 1.0
    entries = jax.random.normal(own_key, extent, jnp.float32) * scale * factor_of
    return jnp.minimum(jnp.maximum(entries, -limit), limit).astype(kind)


def setup_inputs(seed: int = 0) -> dict:
    seeds = jax.random.split(jax.random.key(seed), 8)
    target = draw_target(jax.random.fold_in(seeds[7], 71), 0)
    location = bell_draw(seeds[1], (STEPS, SERIES), 1.0, 6.0, ((0, 4), (1, 8)), jnp.float32)
    variance = jnp.clip(jnp.exp(math.log(4.0) - 2.7725887 * jax.random.uniform(seeds[2], (STEPS, SERIES), jnp.float32) ** steps_of(seeds[2], (STEPS, SERIES), ((0, 4), (1, 8)), -0.2, 0.2)), 0.25, 4.0)
    factor_drift = bell_draw(seeds[3], (STEPS, R, SERIES), (4 * SERIES) ** -0.5, 0.0234375, ((0, 4), (2, 8)))
    loading = draw_loading(jax.random.fold_in(seeds[7], 71), 0)
    node_ids = draw_node_ids(jax.random.fold_in(seeds[7], 71), 0)
    level_weight = jnp.clip(0.5 + 1.5 * jax.random.uniform(seeds[6], (LEVELS, STEPS), jnp.float32) ** steps_of(seeds[6], (LEVELS, STEPS), ((1, 4),), -0.2, 0.2), 0.5, 2.0)
    return dict(target=target, location=location, variance=variance, factor_drift=factor_drift, loading=loading, node_ids=node_ids, level_weight=level_weight)


highest = lax.Precision.HIGHEST

def node_terms(vectors, variance, residual, owned):
    safe_variance = jnp.where(variance > 0.0, variance, 1.0)
    weights = 1.0 / safe_variance
    scaled = vectors * (weights * owned)[:, None, :]
    capacity_part = jnp.einsum('trn,tkn->trk', scaled, vectors, precision=highest)
    projection = jnp.einsum('trn,tn->tr', scaled, residual, precision=highest)
    return (capacity_part, projection, weights)

def level_solve(capacity_sum, projection_sum):
    order_size = capacity_sum.shape[-1]
    identity = jnp.eye(order_size, dtype=jnp.float32)
    capacitance = identity + capacity_sum
    lower_factors = jnp.linalg.cholesky(capacitance)
    inverse = jax.vmap(lambda lower_factor: jax.scipy.linalg.cho_solve((lower_factor, True), identity))(lower_factors)
    coefficient = jnp.einsum('trk,tk->tr', inverse, projection_sum, precision=highest)
    return (inverse, coefficient)

def node_grads(vectors, weights, residual, inverse, coefficient):
    solved = jnp.einsum('trk,tkn->trn', inverse, vectors, precision=highest)
    fitted = jnp.einsum('trn,tr->tn', vectors, coefficient, precision=highest)
    whitened = weights * (residual - fitted)
    leverage = jnp.sum(vectors * solved, axis=1)
    variance_grad = 0.5 * (weights - weights * weights * leverage - whitened * whitened)
    factor_grad = solved * weights[:, None, :] - coefficient[:, :, None] * whitened[:, None, :]
    return (-whitened, variance_grad, factor_grad)

def reference(target, location, variance, factor_drift, loading, node_ids, level_weight):
    slot_count = SERIES // 4 + 1
    static_part = loading.astype(jnp.float32)

    def one_step(step_index):
        vectors = (static_part + factor_drift[step_index].astype(jnp.float32))[None]
        residual = (target[step_index] - location[step_index])[None]
        step_variance = variance[step_index][None]
        weight_row = level_weight[:, step_index]
        capacity_part, projection, weights = node_terms(vectors, step_variance, residual, 1.0)
        inverse, coefficient = level_solve(capacity_part, projection)
        location_grad, variance_grad, factor_grad = node_grads(vectors, weights, residual, inverse, coefficient)
        total_location = weight_row[0] * location_grad[0]
        total_variance = weight_row[0] * variance_grad[0]
        total_factor = weight_row[0] * factor_grad[0]
        for level_index in range(LEVELS - 1):
            member_ids = node_ids[level_index]
            node_vectors = jax.ops.segment_sum(vectors[0].T, member_ids, num_segments=slot_count, indices_are_sorted=True).T[None]
            node_variance = jax.ops.segment_sum(step_variance[0], member_ids, num_segments=slot_count, indices_are_sorted=True)[None]
            node_residual = jax.ops.segment_sum(residual[0], member_ids, num_segments=slot_count, indices_are_sorted=True)[None]
            capacity_part, projection, weights = node_terms(node_vectors, node_variance, node_residual, 1.0)
            inverse, coefficient = level_solve(capacity_part, projection)
            node_location, node_variance_grad, node_factor = node_grads(node_vectors, weights, node_residual, inverse, coefficient)
            weight_now = weight_row[level_index + 1]
            total_location = total_location + weight_now * jnp.take(node_location[0], member_ids, axis=0)
            total_variance = total_variance + weight_now * jnp.take(node_variance_grad[0], member_ids, axis=0)
            total_factor = total_factor + weight_now * jnp.take(node_factor[0], member_ids, axis=1)
        return (total_location, total_variance, total_factor)
    gradient_location, gradient_variance, gradient_drift = lax.map(one_step, jnp.arange(STEPS, dtype=jnp.int32))
    gradient_loading = jnp.sum(gradient_drift, axis=0)
    return (gradient_location, gradient_variance, gradient_drift, gradient_loading)
```

```python
import functools

import jax
import jax.numpy as jnp
from jax import lax
from jax.experimental import pallas as pl
from jax.experimental.pallas import tpu as pltpu
from jax.sharding import PartitionSpec as P

MESH = pl.DeviceIdType.MESH
F32 = jnp.float32
BF16 = jnp.bfloat16
SMALL = 16
NT = (((1,), (1,)), ((), ()))
NN = (((1,), (0,)), ((), ()))
TN = (((0,), (0,)), ((), ()))


def split(x):
    hi = x.astype(BF16)
    return hi, (x - hi.astype(F32)).astype(BF16)


def bdot(a, b, dims):
    return lax.dot_general(a, b, dims, preferred_element_type=F32)


def dot3(a, b, dims):
    ah, al = a
    bh, bl = b
    return bdot(ah, bh, dims) + (bdot(ah, bl, dims) + bdot(al, bh, dims))


def exact(a, b, dims):
    return lax.dot_general(
        a, b, dims, precision=lax.Precision.HIGHEST, preferred_element_type=F32
    )


def invert(a, size):
    lane = lax.broadcasted_iota(jnp.int32, a.shape, 1)
    row = lax.broadcasted_iota(jnp.int32, a.shape, 0)
    for k in range(size):
        pivot = 1.0 / a[k : k + 1, k : k + 1]
        col = a[:, k : k + 1]
        here = lane[:1] == k
        new_row = jnp.where(here, 1.0, a[k : k + 1, :]) * pivot
        rest = jnp.where(lane == k, 0.0, a) - col * new_row
        a = jnp.where(row == k, new_row, rest)
    return a


def kernel(
    n_series, n_tm,
    target_ref, location_ref, variance_ref, drift_ref, loading_ref, ids_ref, weight_ref,
    gloc_ref, gvar_ref, gdrift_ref, gload_ref,
    lbuf, x, hot, v, z, bnd, cs, crecv, invs, g, gs, lsend, lrecv,
    lsem_s, lsem_r, bsem_s, bsem_r, csem_s, csem_r, isem_s, isem_r, gsem_s, gsem_r,
):
    steps, rank, count = drift_ref.shape
    upper = ids_ref.shape[0]
    slots = hot.shape[0]
    wide = rank + 16
    mats = (upper + 1) * steps
    offsets = [0] + [slots - SMALL * (upper - 1 - i) for i in range(upper - 1)]
    part = count // n_tm
    me = lax.axis_index("series")
    mt = lax.axis_index("tm")

    barrier = pltpu.get_barrier_semaphore()

    def hello(k, c):
        pl.semaphore_signal(
            barrier, inc=1, device_id={"series": lax.rem(me + k, n_series)}, device_id_type=MESH
        )
        return c

    lax.fori_loop(1, n_series, hello, 0)
    for k in range(1, n_tm):
        pl.semaphore_signal(
            barrier, inc=1, device_id={"tm": lax.rem(mt + k, n_tm)}, device_id_type=MESH
        )
    pl.semaphore_wait(barrier, n_series - 1 + n_tm - 1)

    loads = []
    for k in range(1, n_tm):
        loads.append(
            pltpu.make_async_remote_copy(
                src_ref=loading_ref, dst_ref=lbuf.at[mt],
                send_sem=lsem_s.at[k], recv_sem=lsem_r.at[k],
                device_id={"tm": lax.rem(mt + k, n_tm)}, device_id_type=MESH,
            )
        )
        loads[-1].start()
    lbuf[mt] = loading_ref[...]

    for u in range(upper):
        size = (offsets[1] if upper > 1 else slots) if u == 0 else SMALL
        member = ids_ref[u : u + 1, :] - ids_ref[u : u + 1, 0:1]
        for at in range(0, size, SMALL * 2 if size % (SMALL * 2) == 0 else SMALL):
            rows = min(SMALL * 2, size)
            slot = lax.broadcasted_iota(jnp.int32, (rows, count), 0) + at
            hot[offsets[u] + at : offsets[u] + at + rows, :] = jnp.where(
                slot == member, 1.0, 0.0
            ).astype(BF16)

    residual = target_ref[...] - location_ref[...]
    variance = variance_ref[...]
    for t in range(steps):
        base = t * wide + rank
        v[base : base + 16, :] = jnp.zeros((16, count), F32)
        v[base : base + steps, :] = variance
        v[base + steps : base + 2 * steps, :] = residual
    aux = v[rank : rank + 8, :]
    one = aux.astype(BF16).astype(F32)
    two = (aux - one).astype(BF16).astype(F32)
    three = aux - one - two
    head = (steps + 1) * rank
    x[head : head + 32, :] = jnp.concatenate([one, two, three, jnp.zeros_like(one)], axis=0).astype(BF16)
    for t in range(steps):
        x[t * rank : (t + 1) * rank, :] = drift_ref[t]

    for copy in loads:
        copy.wait_recv()
    for j in range(n_tm):
        x[steps * rank : head, j * part : (j + 1) * part] = lbuf[j]
    loading = x[steps * rank : head, :].astype(F32)
    for t in range(steps):
        v[t * wide : t * wide + rank, :] = loading + drift_ref[t].astype(F32)

    sums = bdot(x[...], hot[...], NT)
    for t in range(steps):
        z[t * wide : t * wide + rank, :] = sums[t * rank : (t + 1) * rank] + sums[steps * rank : head]
        base = t * wide + rank
        z[base : base + 8, :] = (
            sums[head : head + 8] + sums[head + 8 : head + 16] + sums[head + 16 : head + 24]
        )
        z[base + 8 : base + 16, :] = jnp.zeros((8, slots), F32)

    row8 = lax.broadcasted_iota(jnp.int32, (8, slots), 0)
    slot8 = lax.broadcasted_iota(jnp.int32, (8, slots), 1)
    pick = jnp.zeros((8, slots), F32)
    put = jnp.zeros((8, slots), F32)
    col_row = lax.broadcasted_iota(jnp.int32, (8, 1), 0)
    ids_sent = jnp.full((8, 1), -1.0, F32)
    ids_mine = jnp.full((8, 1), -2.0, F32)
    for u in range(upper):
        first = ids_ref[u : u + 1, 0:1]
        last = ids_ref[u : u + 1, count - 1 : count]
        final = last - first + offsets[u]
        at_first = jnp.where(slot8 == offsets[u], 1.0, 0.0)
        at_last = jnp.where(slot8 == final, 1.0, 0.0)
        pick = jnp.where(row8 == u, at_first, jnp.where(row8 == u + upper, at_last, pick))
        put = jnp.where(row8 == u, at_last, jnp.where(row8 == u + upper, at_first, put))
        first = first.astype(F32)
        last = last.astype(F32)
        ids_sent = jnp.where(col_row == u, first, jnp.where(col_row == u + upper, last, ids_sent))
        ids_mine = jnp.where(col_row == u, last, jnp.where(col_row == u + upper, first, ids_mine))
    lane_p = lax.broadcasted_iota(jnp.int32, (8, steps * wide), 1)
    id_lane = rank + 8
    bnd[me] = jnp.where(lane_p == id_lane, ids_sent, exact(pick, z[...], NT))

    def bnd_copy(k):
        return pltpu.make_async_remote_copy(
            src_ref=bnd.at[me], dst_ref=bnd.at[me], send_sem=bsem_s, recv_sem=bsem_r,
            device_id={"series": lax.rem(me + k, n_series)}, device_id_type=MESH,
        )

    def bnd_start(k, c):
        bnd_copy(k).start()
        return c

    lax.fori_loop(1, n_series, bnd_start, 0)

    def send_matrix(m, value):
        @pl.when(me == m)
        def _():
            crecv[me] = value

        @pl.when(me != m)
        def _():
            cs[m] = value
            pltpu.make_async_remote_copy(
                src_ref=cs.at[m], dst_ref=crecv.at[me], send_sem=csem_s, recv_sem=csem_r,
                device_id={"series": jnp.int32(m)}, device_id_type=MESH,
            ).start()

    for t in range(steps):
        full = v[t * wide : (t + 1) * wide, :]
        weights = 1.0 / variance[t : t + 1]
        send_matrix(t, dot3(split(full[:rank] * weights), split(full), NT))

    many = pltpu.make_async_copy(
        bnd.at[pl.ds(0, n_series - 1)], bnd.at[pl.ds(0, n_series - 1)], bsem_r
    )
    many.wait()

    def join(d, carry):
        total, gate = carry
        theirs = bnd[d]
        higher = jnp.where(d > me, 1.0, 0.0)
        lower = jnp.where(d < me, 1.0, 0.0)
        same = jnp.where(theirs[:, id_lane : id_lane + 1] == ids_mine, 1.0, 0.0)
        mask = same * jnp.where(col_row < upper, higher, lower)
        return total + mask * theirs, jnp.maximum(gate, mask)

    total, gate = lax.fori_loop(
        0, n_series, join, (jnp.zeros((8, steps * wide), F32), jnp.zeros((8, 1), F32))
    )
    total = jnp.where(lane_p == id_lane, 0.0, total)
    z[...] = z[...] + exact(total, put, TN)
    owned = 1.0 - jnp.sum(put * jnp.where(col_row < upper, gate, 0.0), axis=0, keepdims=True)

    slot1 = lax.broadcasted_iota(jnp.int32, (1, slots), 1)
    level_of = jnp.zeros((1, slots), jnp.int32)
    for u in range(1, upper):
        level_of = jnp.where(slot1 >= offsets[u], u, level_of)
    tail = slots - 128
    node_weights = []
    for t in range(steps):
        full = z[t * wide : (t + 1) * wide, :]
        var = full[rank + t : rank + t + 1]
        weights = 1.0 / jnp.where(var > 0.0, var, 1.0)
        node_weights.append(weights)
        scaled = full[:rank] * (weights * owned)
        right = split(full)
        send_matrix(steps + t, dot3(split(jnp.where(level_of == 0, scaled, 0.0)), right, NT))
        end = (right[0][:, tail:], right[1][:, tail:])
        for u in range(1, upper):
            left = jnp.where(level_of[:, tail:] == u, scaled[:, tail:], 0.0)
            send_matrix((u + 1) * steps + t, dot3(split(left), end, NT))

    def inv_copy(k):
        return pltpu.make_async_remote_copy(
            src_ref=invs.at[me], dst_ref=invs.at[me], send_sem=isem_s, recv_sem=isem_r,
            device_id={"series": lax.rem(me + k, n_series)}, device_id_type=MESH,
        )

    def solve():
        pltpu.make_async_copy(
            crecv.at[pl.ds(0, n_series - 1)], crecv.at[pl.ds(0, n_series - 1)], csem_r
        ).wait()
        shape = (rank, wide)
        eye = jnp.where(
            lax.broadcasted_iota(jnp.int32, shape, 0) == lax.broadcasted_iota(jnp.int32, shape, 1), 1.0, 0.0
        )
        a = lax.fori_loop(0, n_series, lambda d, c: c + crecv[d], eye)
        invs[me] = invert(a, rank)

        def start(k, c):
            inv_copy(k).start()
            return c

        lax.fori_loop(1, n_series, start, 0)
        pltpu.make_async_copy(
            invs.at[pl.ds(0, mats - 1)], invs.at[pl.ds(0, mats - 1)], isem_r
        ).wait()

    if n_series == mats:
        solve()
    else:
        pl.when(me < mats)(solve)

        @pl.when(me >= mats)
        def _():
            pltpu.make_async_copy(invs, invs, isem_r).wait()

    g[...] = jnp.zeros_like(g)
    for t in range(steps):
        full = z[t * wide : (t + 1) * wide, :]
        vec = full[:rank]
        weights = node_weights[t]
        res = full[rank + steps + t : rank + steps + t + 1]
        c = rank + steps + t
        parts = split(vec)
        end = (parts[0][:, tail:], parts[1][:, tail:])
        first = invs[steps + t]
        solved = dot3(split(first[:, :rank]), parts, NN)
        solved_end = solved[:, tail:]
        coef = jnp.broadcast_to(first[:, c : c + 1], (rank, slots))
        scale = jnp.broadcast_to(weight_ref[1:2, t : t + 1], (1, slots))
        for u in range(1, upper):
            inv = invs[(u + 1) * steps + t]
            here = level_of[:, tail:] == u
            solved_end = jnp.where(here, dot3(split(inv[:, :rank]), end, NN), solved_end)
            coef = jnp.where(level_of == u, inv[:, c : c + 1], coef)
            scale = jnp.where(level_of == u, weight_ref[u + 1 : u + 2, t : t + 1], scale)
        solved = jnp.concatenate([solved[:, :tail], solved_end], axis=1)
        fitted = jnp.sum(vec * coef, axis=0, keepdims=True)
        white = weights * (res - fitted)
        leverage = jnp.sum(vec * solved, axis=0, keepdims=True)
        base = steps * rank
        g[t * rank : (t + 1) * rank, :] = scale * (solved * weights - coef * white)
        g[base + t : base + t + 1, :] = -scale * white
        g[base + steps + t : base + steps + t + 1, :] = (
            scale * 0.5 * (weights - weights * weights * leverage - white * white)
        )
    ghi, glo = split(g[...])
    height = g.shape[0]
    gs[:height, :] = ghi
    gs[height:, :] = glo

    inv_parts = [split(invs[t][:, :rank]) for t in range(steps)]
    copies = []
    for k in list(range(1, n_tm)) + [0]:
        j = lax.rem(mt + k, n_tm)
        cols = pl.ds(pl.multiple_of(j * part, part), part)
        both = bdot(gs[...], hot[:, cols], NN)
        up = both[:height] + both[height:]
        loading_sum = None
        for t in range(steps):
            c = rank + steps + t
            vec = v[t * wide : t * wide + rank, cols]
            var = v[rank + t : rank + t + 1, cols]
            res = v[rank + steps + t : rank + steps + t + 1, cols]
            weights = 1.0 / var
            coef = invs[t][:, c : c + 1]
            scale = weight_ref[0:1, t : t + 1]
            solved = dot3(inv_parts[t], split(vec), NN)
            fitted = jnp.sum(vec * coef, axis=0, keepdims=True)
            white = weights * (res - fitted)
            leverage = jnp.sum(vec * solved, axis=0, keepdims=True)
            base = steps * rank
            drift = up[t * rank : (t + 1) * rank] + scale * (solved * weights - coef * white)
            gdrift_ref[t, :, cols] = drift
            gloc_ref[t : t + 1, cols] = up[base + t : base + t + 1] - scale * white
            gvar_ref[t : t + 1, cols] = up[base + steps + t : base + steps + t + 1] + scale * 0.5 * (
                weights - weights * weights * leverage - white * white
            )
            loading_sum = drift if loading_sum is None else loading_sum + drift
        if k:
            lsend[k] = loading_sum
            copy = pltpu.make_async_remote_copy(
                src_ref=lsend.at[k], dst_ref=lrecv.at[k],
                send_sem=gsem_s.at[k], recv_sem=gsem_r.at[k],
                device_id={"tm": j}, device_id_type=MESH,
            )
            copy.start()
            copies.append(copy)
    for k, copy in zip(range(1, n_tm), copies):
        copy.wait_recv()
        loading_sum = loading_sum + lrecv[k]
    gload_ref[...] = loading_sum

    for copy in loads + copies:
        copy.wait_send()
    pltpu.make_async_copy(
        bnd.at[pl.ds(0, n_series - 1)], bnd.at[pl.ds(0, n_series - 1)], bsem_s
    ).wait()

    def sent(own):
        held = cs.at[pl.ds(0, mats - 1 if own else mats)]
        pltpu.make_async_copy(held, held, csem_s).wait()
        if own:
            pltpu.make_async_copy(
                crecv.at[pl.ds(0, n_series - 1)], crecv.at[pl.ds(0, n_series - 1)], isem_s
            ).wait()

    if n_series == mats:
        sent(True)
    else:
        pl.when(me < mats)(functools.partial(sent, True))
        pl.when(me >= mats)(functools.partial(sent, False))


def local(target, location, variance, factor_drift, loading, node_ids, level_weight):
    steps, rank, count = factor_drift.shape
    upper = node_ids.shape[0]
    n_series, n_tm = lax.axis_size("series"), lax.axis_size("tm")
    slots = count // 4
    part = count // n_tm
    wide = rank + 16
    mats = (upper + 1) * steps
    height = steps * rank + 16
    vmem = pl.BlockSpec(memory_space=pltpu.VMEM)
    dma = pltpu.SemaphoreType.DMA
    return pl.pallas_call(
        functools.partial(kernel, n_series, n_tm),
        out_shape=(
            jax.ShapeDtypeStruct((steps, count), F32),
            jax.ShapeDtypeStruct((steps, count), F32),
            jax.ShapeDtypeStruct((steps, rank, count), F32),
            jax.ShapeDtypeStruct((rank, part), F32),
        ),
        in_specs=[vmem] * 7,
        out_specs=(vmem,) * 4,
        scratch_shapes=[
            pltpu.VMEM((n_tm, rank, part), BF16),
            pltpu.VMEM(((steps + 1) * rank + 32, count), BF16),
            pltpu.VMEM((slots, count), BF16),
            pltpu.VMEM((steps * wide, count), F32),
            pltpu.VMEM((steps * wide, slots), F32),
            pltpu.VMEM((n_series, 8, steps * wide), F32),
            pltpu.VMEM((mats, rank, wide), F32),
            pltpu.VMEM((n_series, rank, wide), F32),
            pltpu.VMEM((mats, rank, wide), F32),
            pltpu.VMEM((height, slots), F32),
            pltpu.VMEM((2 * height, slots), BF16),
            pltpu.VMEM((n_tm, rank, part), F32),
            pltpu.VMEM((n_tm, rank, part), F32),
            dma((n_tm,)), dma((n_tm,)),
            dma, dma, dma, dma, dma, dma,
            dma((n_tm,)), dma((n_tm,)),
        ],
        compiler_params=pltpu.CompilerParams(
            collective_id=0, has_side_effects=True, vmem_limit_bytes=48 * 1024 * 1024
        ),
    )(target, location, variance, factor_drift, loading, node_ids, level_weight)


def solution(mesh):
    return jax.shard_map(
        local,
        mesh=mesh,
        in_specs=(
            P("tm", "series"),
            P("tm", "series"),
            P("tm", "series"),
            P("tm", None, "series"),
            P(None, ("series", "tm")),
            P(None, "series"),
            P(None, "tm"),
        ),
        out_specs=(
            P("tm", "series"),
            P("tm", "series"),
            P("tm", None, "series"),
            P(None, ("series", "tm")),
        ),
        check_vma=False,
    )
```

```python
import functools

import jax
import jax.numpy as jnp
from jax import lax
from jax.experimental import pallas as pl
from jax.experimental.pallas import tpu as pltpu
from jax.sharding import PartitionSpec as P

MESH = pl.DeviceIdType.MESH
F32 = jnp.float32
BF16 = jnp.bfloat16
SMALL = 16
NT = (((1,), (1,)), ((), ()))
NN = (((1,), (0,)), ((), ()))
TN = (((0,), (0,)), ((), ()))


def split(x):
    hi = x.astype(BF16)
    return hi, (x - hi.astype(F32)).astype(BF16)


def bdot(a, b, dims):
    return lax.dot_general(a, b, dims, preferred_element_type=F32)


def dot3(a, b, dims):
    ah, al = a
    bh, bl = b
    return bdot(ah, bh, dims) + (bdot(ah, bl, dims) + bdot(al, bh, dims))


def exact(a, b, dims):
    return lax.dot_general(
        a, b, dims, precision=lax.Precision.HIGHEST, preferred_element_type=F32
    )


def pack(value, rank):
    half = rank // 2
    left = jnp.concatenate([value[:half, :rank], value[rank : rank + 8, :rank]], axis=0)
    right = jnp.concatenate([value[half:rank, :rank], jnp.zeros((8, rank), F32)], axis=0)
    return jnp.concatenate([left, right], axis=1)


def unpack(packed):
    half, rank = packed.shape[0] - 8, packed.shape[1] // 2
    matrix = jnp.concatenate([packed[:half, :rank], packed[:half, rank:]], axis=0)
    return matrix, packed[half:]


def invert(a, size):
    lane = lax.broadcasted_iota(jnp.int32, a.shape, 1)
    row = lax.broadcasted_iota(jnp.int32, a.shape, 0)
    for k in range(size):
        pivot = 1.0 / a[k : k + 1, k : k + 1]
        col = a[:, k : k + 1]
        here = lane[:1] == k
        new_row = jnp.where(here, 1.0, a[k : k + 1, :]) * pivot
        rest = jnp.where(lane == k, 0.0, a) - col * new_row
        a = jnp.where(row == k, new_row, rest)
    return a


def kernel(
    n_series, n_tm,
    target_hbm, location_hbm, variance_hbm, drift_hbm, loading_hbm, ids_hbm, weight_hbm,
    gloc_ref, gvar_ref, gdrift_ref, gload_ref,
    target_ref, location_ref, variance_ref, drift_ref, loading_ref, ids_ref, weight_ref, in_sem,
    lbuf, x, hot, v, z, bnd, cs, crecv, invs, g, gs, lsend, lrecv,
    lsem_s, lsem_r, bsem_s, bsem_r, csem_s, csem_r, isem_s, isem_r, gsem_s, gsem_r,
):
    steps, rank, count = drift_hbm.shape
    upper = ids_hbm.shape[0]
    slots = hot.shape[0]
    wide = rank + 16
    mats = (upper + 1) * steps
    offsets = [0] + [slots - SMALL * (upper - 1 - i) for i in range(upper - 1)]
    part = count // n_tm
    me = lax.axis_index("series")
    mt = lax.axis_index("tm")

    barrier = pltpu.get_barrier_semaphore()
    ins = [
        pltpu.make_async_copy(src, dst, in_sem.at[i])
        for i, (src, dst) in enumerate((
            (loading_hbm, loading_ref), (ids_hbm, ids_ref), (target_hbm, target_ref),
            (location_hbm, location_ref), (variance_hbm, variance_ref),
            (drift_hbm, drift_ref), (weight_hbm, weight_ref),
        ))
    ]
    for copy in ins:
        copy.start()

    def hello(k, c):
        pl.semaphore_signal(
            barrier, inc=1, device_id={"series": lax.rem(me + k, n_series)}, device_id_type=MESH
        )
        return c

    lax.fori_loop(1, n_series, hello, 0)
    for k in range(1, n_tm):
        pl.semaphore_signal(
            barrier, inc=1, device_id={"tm": lax.rem(mt + k, n_tm)}, device_id_type=MESH
        )
    pl.semaphore_wait(barrier, n_series - 1 + n_tm - 1)

    loads = []
    ins[0].wait()
    for k in range(1, n_tm):
        loads.append(
            pltpu.make_async_remote_copy(
                src_ref=loading_ref, dst_ref=lbuf.at[mt],
                send_sem=lsem_s.at[k], recv_sem=lsem_r.at[k],
                device_id={"tm": lax.rem(mt + k, n_tm)}, device_id_type=MESH,
            )
        )
        loads[-1].start()
    lbuf[mt] = loading_ref[...]

    ins[1].wait()
    for u in range(upper):
        size = (offsets[1] if upper > 1 else slots) if u == 0 else SMALL
        member = ids_ref[u : u + 1, :] - ids_ref[u : u + 1, 0:1]
        for at in range(0, size, SMALL * 2 if size % (SMALL * 2) == 0 else SMALL):
            rows = min(SMALL * 2, size)
            slot = lax.broadcasted_iota(jnp.int32, (rows, count), 0) + at
            hot[offsets[u] + at : offsets[u] + at + rows, :] = jnp.where(
                slot == member, 1.0, 0.0
            ).astype(BF16)

    for copy in ins[2:]:
        copy.wait()
    residual = target_ref[...] - location_ref[...]
    variance = variance_ref[...]
    for t in range(steps):
        base = t * wide + rank
        v[base : base + 16, :] = jnp.zeros((16, count), F32)
        v[base : base + steps, :] = variance
        v[base + steps : base + 2 * steps, :] = residual
    aux = v[rank : rank + 8, :]
    one = aux.astype(BF16).astype(F32)
    two = (aux - one).astype(BF16).astype(F32)
    three = aux - one - two
    head = (steps + 1) * rank
    x[head : head + 32, :] = jnp.concatenate([one, two, three, jnp.zeros_like(one)], axis=0).astype(BF16)
    for t in range(steps):
        x[t * rank : (t + 1) * rank, :] = drift_ref[t]

    for copy in loads:
        copy.wait_recv()
    for j in range(n_tm):
        x[steps * rank : head, j * part : (j + 1) * part] = lbuf[j]
    loading = x[steps * rank : head, :].astype(F32)
    for t in range(steps):
        v[t * wide : t * wide + rank, :] = loading + drift_ref[t].astype(F32)

    sums = bdot(x[...], hot[...], NT)
    for t in range(steps):
        z[t * wide : t * wide + rank, :] = sums[t * rank : (t + 1) * rank] + sums[steps * rank : head]
        base = t * wide + rank
        z[base : base + 8, :] = (
            sums[head : head + 8] + sums[head + 8 : head + 16] + sums[head + 16 : head + 24]
        )
        z[base + 8 : base + 16, :] = jnp.zeros((8, slots), F32)

    row8 = lax.broadcasted_iota(jnp.int32, (8, slots), 0)
    slot8 = lax.broadcasted_iota(jnp.int32, (8, slots), 1)
    pick = jnp.zeros((8, slots), F32)
    put = jnp.zeros((8, slots), F32)
    col_row = lax.broadcasted_iota(jnp.int32, (8, 1), 0)
    ids_sent = jnp.full((8, 1), -1.0, F32)
    ids_mine = jnp.full((8, 1), -2.0, F32)
    for u in range(upper):
        first = ids_ref[u : u + 1, 0:1]
        last = ids_ref[u : u + 1, count - 1 : count]
        final = last - first + offsets[u]
        at_first = jnp.where(slot8 == offsets[u], 1.0, 0.0)
        at_last = jnp.where(slot8 == final, 1.0, 0.0)
        pick = jnp.where(row8 == u, at_first, jnp.where(row8 == u + upper, at_last, pick))
        put = jnp.where(row8 == u, at_last, jnp.where(row8 == u + upper, at_first, put))
        first = first.astype(F32)
        last = last.astype(F32)
        ids_sent = jnp.where(col_row == u, first, jnp.where(col_row == u + upper, last, ids_sent))
        ids_mine = jnp.where(col_row == u, last, jnp.where(col_row == u + upper, first, ids_mine))
    lane_p = lax.broadcasted_iota(jnp.int32, (8, steps * wide), 1)
    id_lane = rank + 8
    bnd[me] = jnp.where(lane_p == id_lane, ids_sent, exact(pick, z[...], NT))

    def bnd_copy(k):
        return pltpu.make_async_remote_copy(
            src_ref=bnd.at[me], dst_ref=bnd.at[me], send_sem=bsem_s, recv_sem=bsem_r,
            device_id={"series": lax.rem(me + k, n_series)}, device_id_type=MESH,
        )

    def bnd_start(k, c):
        bnd_copy(k).start()
        return c

    lax.fori_loop(1, n_series, bnd_start, 0)

    def send_matrix(m, whole):
        value = pack(whole, rank)

        @pl.when(me == m)
        def _():
            crecv[me] = value

        @pl.when(me != m)
        def _():
            cs[m] = value
            pltpu.make_async_remote_copy(
                src_ref=cs.at[m], dst_ref=crecv.at[me], send_sem=csem_s, recv_sem=csem_r,
                device_id={"series": jnp.int32(m)}, device_id_type=MESH,
            ).start()

    for t in range(steps):
        full = v[t * wide : (t + 1) * wide, :]
        weights = 1.0 / variance[t : t + 1]
        send_matrix(t, dot3(split(full * weights), split(full), NT))

    many = pltpu.make_async_copy(
        bnd.at[pl.ds(0, n_series - 1)], bnd.at[pl.ds(0, n_series - 1)], bsem_r
    )
    many.wait()

    def join(d, carry):
        total, gate = carry
        theirs = bnd[d]
        higher = jnp.where(d > me, 1.0, 0.0)
        lower = jnp.where(d < me, 1.0, 0.0)
        same = jnp.where(theirs[:, id_lane : id_lane + 1] == ids_mine, 1.0, 0.0)
        mask = same * jnp.where(col_row < upper, higher, lower)
        return total + mask * theirs, jnp.maximum(gate, mask)

    total, gate = lax.fori_loop(
        0, n_series, join, (jnp.zeros((8, steps * wide), F32), jnp.zeros((8, 1), F32))
    )
    total = jnp.where(lane_p == id_lane, 0.0, total)
    z[...] = z[...] + exact(total, put, TN)
    owned = 1.0 - jnp.sum(put * jnp.where(col_row < upper, gate, 0.0), axis=0, keepdims=True)

    slot1 = lax.broadcasted_iota(jnp.int32, (1, slots), 1)
    level_of = jnp.zeros((1, slots), jnp.int32)
    for u in range(1, upper):
        level_of = jnp.where(slot1 >= offsets[u], u, level_of)
    tail = slots - 128
    node_weights = []
    for t in range(steps):
        full = z[t * wide : (t + 1) * wide, :]
        var = full[rank + t : rank + t + 1]
        weights = 1.0 / jnp.where(var > 0.0, var, 1.0)
        node_weights.append(weights)
        scaled = full * (weights * owned)
        right = split(full)
        send_matrix(steps + t, dot3(split(jnp.where(level_of == 0, scaled, 0.0)), right, NT))
        end = (right[0][:, tail:], right[1][:, tail:])
        for u in range(1, upper):
            left = jnp.where(level_of[:, tail:] == u, scaled[:, tail:], 0.0)
            send_matrix((u + 1) * steps + t, dot3(split(left), end, NT))

    def inv_copy(k):
        return pltpu.make_async_remote_copy(
            src_ref=invs.at[me], dst_ref=invs.at[me], send_sem=isem_s, recv_sem=isem_r,
            device_id={"series": lax.rem(me + k, n_series)}, device_id_type=MESH,
        )

    def solve():
        pltpu.make_async_copy(
            crecv.at[pl.ds(0, n_series - 1)], crecv.at[pl.ds(0, n_series - 1)], csem_r
        ).wait()
        shape = (rank, rank)
        eye = jnp.where(
            lax.broadcasted_iota(jnp.int32, shape, 0) == lax.broadcasted_iota(jnp.int32, shape, 1), 1.0, 0.0
        )
        a, below = unpack(lax.fori_loop(1, n_series, lambda d, c: c + crecv[d], crecv[0]))
        a = invert(a + eye, rank)
        invs[me] = pack(jnp.concatenate([a, exact(below[:, :rank], a, NN)], axis=0), rank)

        def start(k, c):
            inv_copy(k).start()
            return c

        lax.fori_loop(1, n_series, start, 0)
        pltpu.make_async_copy(
            invs.at[pl.ds(0, mats - 1)], invs.at[pl.ds(0, mats - 1)], isem_r
        ).wait()

    if n_series == mats:
        solve()
    else:
        pl.when(me < mats)(solve)

        @pl.when(me >= mats)
        def _():
            pltpu.make_async_copy(invs, invs, isem_r).wait()

    inverses, coefs = [], []
    for m in range(mats):
        matrix, below = unpack(invs[m])
        inverses.append(split(matrix))
        c = steps + m % steps
        coefs.append(below.T[:rank, c : c + 1])

    g[...] = jnp.zeros_like(g)
    for t in range(steps):
        full = z[t * wide : (t + 1) * wide, :]
        vec = full[:rank]
        weights = node_weights[t]
        res = full[rank + steps + t : rank + steps + t + 1]
        parts = split(vec)
        end = (parts[0][:, tail:], parts[1][:, tail:])
        solved = dot3(inverses[steps + t], parts, NN)
        solved_end = solved[:, tail:]
        coef = jnp.broadcast_to(coefs[steps + t], (rank, slots))
        scale = jnp.broadcast_to(weight_ref[t : t + 1, 1:2], (1, slots))
        for u in range(1, upper):
            m = (u + 1) * steps + t
            here = level_of[:, tail:] == u
            solved_end = jnp.where(here, dot3(inverses[m], end, NN), solved_end)
            coef = jnp.where(level_of == u, coefs[m], coef)
            scale = jnp.where(level_of == u, weight_ref[t : t + 1, u + 1 : u + 2], scale)
        solved = jnp.concatenate([solved[:, :tail], solved_end], axis=1)
        fitted = jnp.sum(vec * coef, axis=0, keepdims=True)
        white = weights * (res - fitted)
        leverage = jnp.sum(vec * solved, axis=0, keepdims=True)
        base = steps * rank
        g[t * rank : (t + 1) * rank, :] = scale * (solved * weights - coef * white)
        g[base + t : base + t + 1, :] = -scale * white
        g[base + steps + t : base + steps + t + 1, :] = (
            scale * 0.5 * (weights - weights * weights * leverage - white * white)
        )
    ghi, glo = split(g[...])
    height = g.shape[0]
    gs[:height, :] = ghi
    gs[height:, :] = glo

    copies = []
    for k in list(range(1, n_tm)) + [0]:
        j = lax.rem(mt + k, n_tm)
        cols = pl.ds(pl.multiple_of(j * part, part), part)
        both = bdot(gs[...], hot[:, cols], NN)
        up = both[:height] + both[height:]
        loading_sum = None
        for t in range(steps):
            vec = v[t * wide : t * wide + rank, cols]
            var = v[rank + t : rank + t + 1, cols]
            res = v[rank + steps + t : rank + steps + t + 1, cols]
            weights = 1.0 / var
            coef = coefs[t]
            scale = weight_ref[t : t + 1, 0:1]
            solved = dot3(inverses[t], split(vec), NN)
            fitted = jnp.sum(vec * coef, axis=0, keepdims=True)
            white = weights * (res - fitted)
            leverage = jnp.sum(vec * solved, axis=0, keepdims=True)
            base = steps * rank
            drift = up[t * rank : (t + 1) * rank] + scale * (solved * weights - coef * white)
            gdrift_ref[t, :, cols] = drift
            gloc_ref[t : t + 1, cols] = up[base + t : base + t + 1] - scale * white
            gvar_ref[t : t + 1, cols] = up[base + steps + t : base + steps + t + 1] + scale * 0.5 * (
                weights - weights * weights * leverage - white * white
            )
            loading_sum = drift if loading_sum is None else loading_sum + drift
        if k:
            lsend[k] = loading_sum
            copy = pltpu.make_async_remote_copy(
                src_ref=lsend.at[k], dst_ref=lrecv.at[k],
                send_sem=gsem_s.at[k], recv_sem=gsem_r.at[k],
                device_id={"tm": j}, device_id_type=MESH,
            )
            copy.start()
            copies.append(copy)
    for k, copy in zip(range(1, n_tm), copies):
        copy.wait_recv()
        loading_sum = loading_sum + lrecv[k]
    gload_ref[...] = loading_sum

    for copy in loads + copies:
        copy.wait_send()
    pltpu.make_async_copy(
        bnd.at[pl.ds(0, n_series - 1)], bnd.at[pl.ds(0, n_series - 1)], bsem_s
    ).wait()

    def sent(own):
        held = cs.at[pl.ds(0, mats - 1 if own else mats)]
        pltpu.make_async_copy(held, held, csem_s).wait()
        if own:
            pltpu.make_async_copy(
                crecv.at[pl.ds(0, n_series - 1)], crecv.at[pl.ds(0, n_series - 1)], isem_s
            ).wait()

    if n_series == mats:
        sent(True)
    else:
        pl.when(me < mats)(functools.partial(sent, True))
        pl.when(me >= mats)(functools.partial(sent, False))


def local(target, location, variance, factor_drift, loading, node_ids, level_weight):
    steps, rank, count = factor_drift.shape
    upper = node_ids.shape[0]
    n_series, n_tm = lax.axis_size("series"), lax.axis_size("tm")
    slots = count // 4
    part = count // n_tm
    wide = rank + 16
    mats = (upper + 1) * steps
    height = steps * rank + 16
    vmem = pl.BlockSpec(memory_space=pltpu.VMEM)
    dma = pltpu.SemaphoreType.DMA
    operands = (target, location, variance, factor_drift, loading, node_ids, level_weight.T)
    operands = [pltpu.with_memory_space_constraint(a, pltpu.HBM) for a in operands]
    return pl.pallas_call(
        functools.partial(kernel, n_series, n_tm),
        out_shape=(
            jax.ShapeDtypeStruct((steps, count), F32),
            jax.ShapeDtypeStruct((steps, count), F32),
            jax.ShapeDtypeStruct((steps, rank, count), F32),
            jax.ShapeDtypeStruct((rank, part), F32),
        ),
        in_specs=[pl.BlockSpec(memory_space=pltpu.HBM)] * 7,
        out_specs=(vmem,) * 4,
        scratch_shapes=[
            pltpu.VMEM((steps, count), F32),
            pltpu.VMEM((steps, count), F32),
            pltpu.VMEM((steps, count), F32),
            pltpu.VMEM((steps, rank, count), BF16),
            pltpu.VMEM((rank, part), BF16),
            pltpu.VMEM((upper, count), jnp.int32),
            pltpu.VMEM((steps, upper + 1), F32),
            dma((7,)),
            pltpu.VMEM((n_tm, rank, part), BF16),
            pltpu.VMEM(((steps + 1) * rank + 32, count), BF16),
            pltpu.VMEM((slots, count), BF16),
            pltpu.VMEM((steps * wide, count), F32),
            pltpu.VMEM((steps * wide, slots), F32),
            pltpu.VMEM((n_series, 8, steps * wide), F32),
            pltpu.VMEM((mats, rank // 2 + 8, 2 * rank), F32),
            pltpu.VMEM((n_series, rank // 2 + 8, 2 * rank), F32),
            pltpu.VMEM((mats, rank // 2 + 8, 2 * rank), F32),
            pltpu.VMEM((height, slots), F32),
            pltpu.VMEM((2 * height, slots), BF16),
            pltpu.VMEM((n_tm, rank, part), F32),
            pltpu.VMEM((n_tm, rank, part), F32),
            dma((n_tm,)), dma((n_tm,)),
            dma, dma, dma, dma, dma, dma,
            dma((n_tm,)), dma((n_tm,)),
        ],
        compiler_params=pltpu.CompilerParams(
            collective_id=0, has_side_effects=True, vmem_limit_bytes=48 * 1024 * 1024
        ),
    )(*operands)


def solution(mesh):
    return jax.shard_map(
        local,
        mesh=mesh,
        in_specs=(
            P("tm", "series"),
            P("tm", "series"),
            P("tm", "series"),
            P("tm", None, "series"),
            P(None, ("series", "tm")),
            P(None, "series"),
            P(None, "tm"),
        ),
        out_specs=(
            P("tm", "series"),
            P("tm", "series"),
            P("tm", None, "series"),
            P(None, ("series", "tm")),
        ),
        check_vma=False,
    )
```

```python
import functools

import jax
import jax.numpy as jnp
from jax import lax
from jax.experimental import pallas as pl
from jax.experimental.pallas import tpu as pltpu
from jax.sharding import PartitionSpec as P

MESH = pl.DeviceIdType.MESH
F32 = jnp.float32
BF16 = jnp.bfloat16
SMALL = 16
NT = (((1,), (1,)), ((), ()))
NN = (((1,), (0,)), ((), ()))
TN = (((0,), (0,)), ((), ()))


def split(x):
    hi = x.astype(BF16)
    return hi, (x - hi.astype(F32)).astype(BF16)


def bdot(a, b, dims):
    return lax.dot_general(a, b, dims, preferred_element_type=F32)


def dot3(a, b, dims):
    ah, al = a
    bh, bl = b
    return bdot(ah, bh, dims) + (bdot(ah, bl, dims) + bdot(al, bh, dims))


def exact(a, b, dims):
    return lax.dot_general(
        a, b, dims, precision=lax.Precision.HIGHEST, preferred_element_type=F32
    )


def pack(value, rank):
    half = rank // 2
    left = jnp.concatenate([value[:half, :rank], value[rank : rank + 8, :rank]], axis=0)
    right = jnp.concatenate([value[half:rank, :rank], jnp.zeros((8, rank), F32)], axis=0)
    return jnp.concatenate([left, right], axis=1)


def unpack(packed):
    half, rank = packed.shape[0] - 8, packed.shape[1] // 2
    matrix = jnp.concatenate([packed[:half, :rank], packed[:half, rank:]], axis=0)
    return matrix, packed[half:]


def invert(a, size):
    lane = lax.broadcasted_iota(jnp.int32, a.shape, 1)
    row = lax.broadcasted_iota(jnp.int32, a.shape, 0)
    for k in range(size):
        pivot = 1.0 / a[k : k + 1, k : k + 1]
        col = a[:, k : k + 1]
        here = lane[:1] == k
        new_row = jnp.where(here, 1.0, a[k : k + 1, :]) * pivot
        rest = jnp.where(lane == k, 0.0, a) - col * new_row
        a = jnp.where(row == k, new_row, rest)
    return a


def kernel(
    n_series, n_tm,
    target_hbm, location_hbm, variance_hbm, drift_hbm, loading_hbm, ids_hbm, weight_hbm,
    gloc_ref, gvar_ref, gdrift_ref, gload_ref,
    target_ref, location_ref, variance_ref, drift_ref, loading_ref, ids_ref, weight_ref, in_sem,
    lbuf, x, hot, v, z, bnd, cs, crecv, invs, g, gs, lsend, lrecv,
    lsem_s, lsem_r, bsem_s, bsem_r, csem_s, csem_r, isem_s, isem_r, gsem_s, gsem_r,
):
    steps, rank, count = drift_hbm.shape
    upper = ids_hbm.shape[0]
    slots = hot.shape[0]
    wide = rank + 16
    mats = (upper + 1) * steps
    offsets = [0] + [slots - SMALL * (upper - 1 - i) for i in range(upper - 1)]
    part = count // n_tm
    me = lax.axis_index("series")
    mt = lax.axis_index("tm")

    barrier = pltpu.get_barrier_semaphore()
    ins = [
        pltpu.make_async_copy(src, dst, in_sem.at[i])
        for i, (src, dst) in enumerate((
            (loading_hbm, loading_ref), (ids_hbm, ids_ref), (target_hbm, target_ref),
            (location_hbm, location_ref), (variance_hbm, variance_ref),
            (drift_hbm, drift_ref), (weight_hbm, weight_ref),
        ))
    ]
    for copy in ins:
        copy.start()

    def hello(k, c):
        pl.semaphore_signal(
            barrier, inc=1, device_id={"series": lax.rem(me + k, n_series)}, device_id_type=MESH
        )
        return c

    lax.fori_loop(1, n_series, hello, 0)
    for k in range(1, n_tm):
        pl.semaphore_signal(
            barrier, inc=1, device_id={"tm": lax.rem(mt + k, n_tm)}, device_id_type=MESH
        )
    pl.semaphore_wait(barrier, n_series - 1 + n_tm - 1)

    loads = []
    ins[0].wait()
    for k in range(1, n_tm):
        loads.append(
            pltpu.make_async_remote_copy(
                src_ref=loading_ref, dst_ref=lbuf.at[mt],
                send_sem=lsem_s.at[k], recv_sem=lsem_r.at[k],
                device_id={"tm": lax.rem(mt + k, n_tm)}, device_id_type=MESH,
            )
        )
        loads[-1].start()
    lbuf[mt] = loading_ref[...]

    ins[1].wait()
    for u in range(upper):
        size = (offsets[1] if upper > 1 else slots) if u == 0 else SMALL
        member = ids_ref[u : u + 1, :] - ids_ref[u : u + 1, 0:1]
        for at in range(0, size, SMALL * 2 if size % (SMALL * 2) == 0 else SMALL):
            rows = min(SMALL * 2, size)
            slot = lax.broadcasted_iota(jnp.int32, (rows, count), 0) + at
            hot[offsets[u] + at : offsets[u] + at + rows, :] = jnp.where(
                slot == member, 1.0, 0.0
            ).astype(BF16)

    for copy in ins[2:]:
        copy.wait()
    residual = target_ref[...] - location_ref[...]
    variance = variance_ref[...]
    for t in range(steps):
        base = t * wide + rank
        v[base : base + 16, :] = jnp.zeros((16, count), F32)
        v[base : base + steps, :] = variance
        v[base + steps : base + 2 * steps, :] = residual
    aux = v[rank : rank + 8, :]
    one = aux.astype(BF16).astype(F32)
    two = (aux - one).astype(BF16).astype(F32)
    three = aux - one - two
    head = (steps + 1) * rank
    x[head : head + 32, :] = jnp.concatenate([one, two, three, jnp.zeros_like(one)], axis=0).astype(BF16)
    for t in range(steps):
        x[t * rank : (t + 1) * rank, :] = drift_ref[t]

    for copy in loads:
        copy.wait_recv()
    for j in range(n_tm):
        x[steps * rank : head, j * part : (j + 1) * part] = lbuf[j]
    loading = x[steps * rank : head, :].astype(F32)
    for t in range(steps):
        v[t * wide : t * wide + rank, :] = loading + drift_ref[t].astype(F32)

    sums = bdot(x[...], hot[...], NT)
    for t in range(steps):
        z[t * wide : t * wide + rank, :] = sums[t * rank : (t + 1) * rank] + sums[steps * rank : head]
        base = t * wide + rank
        z[base : base + 8, :] = (
            sums[head : head + 8] + sums[head + 8 : head + 16] + sums[head + 16 : head + 24]
        )
        z[base + 8 : base + 16, :] = jnp.zeros((8, slots), F32)

    row8 = lax.broadcasted_iota(jnp.int32, (8, slots), 0)
    slot8 = lax.broadcasted_iota(jnp.int32, (8, slots), 1)
    pick = jnp.zeros((8, slots), F32)
    put = jnp.zeros((8, slots), F32)
    col_row = lax.broadcasted_iota(jnp.int32, (8, 1), 0)
    ids_sent = jnp.full((8, 1), -1.0, F32)
    ids_mine = jnp.full((8, 1), -2.0, F32)
    for u in range(upper):
        first = ids_ref[u : u + 1, 0:1]
        last = ids_ref[u : u + 1, count - 1 : count]
        final = last - first + offsets[u]
        at_first = jnp.where(slot8 == offsets[u], 1.0, 0.0)
        at_last = jnp.where(slot8 == final, 1.0, 0.0)
        pick = jnp.where(row8 == u, at_first, jnp.where(row8 == u + upper, at_last, pick))
        put = jnp.where(row8 == u, at_last, jnp.where(row8 == u + upper, at_first, put))
        first = first.astype(F32)
        last = last.astype(F32)
        ids_sent = jnp.where(col_row == u, first, jnp.where(col_row == u + upper, last, ids_sent))
        ids_mine = jnp.where(col_row == u, last, jnp.where(col_row == u + upper, first, ids_mine))
    lane_p = lax.broadcasted_iota(jnp.int32, (8, steps * wide), 1)
    id_lane = rank + 8
    bnd[me] = jnp.where(lane_p == id_lane, ids_sent, exact(pick, z[...], NT))

    def bnd_copy(k):
        return pltpu.make_async_remote_copy(
            src_ref=bnd.at[me], dst_ref=bnd.at[me], send_sem=bsem_s, recv_sem=bsem_r,
            device_id={"series": lax.rem(me + k, n_series)}, device_id_type=MESH,
        )

    def bnd_start(k, c):
        bnd_copy(k).start()
        return c

    lax.fori_loop(1, n_series, bnd_start, 0)

    def send_matrix(m, whole):
        value = pack(whole, rank)

        @pl.when(me == m)
        def _():
            crecv[me] = value

        @pl.when(me != m)
        def _():
            cs[m] = value
            pltpu.make_async_remote_copy(
                src_ref=cs.at[m], dst_ref=crecv.at[me], send_sem=csem_s, recv_sem=csem_r,
                device_id={"series": jnp.int32(m)}, device_id_type=MESH,
            ).start()

    for t in range(steps):
        full = v[t * wide : (t + 1) * wide, :]
        weights = 1.0 / variance[t : t + 1]
        send_matrix(t, dot3(split(full * weights), split(full), NT))

    many = pltpu.make_async_copy(
        bnd.at[pl.ds(0, n_series - 1)], bnd.at[pl.ds(0, n_series - 1)], bsem_r
    )
    many.wait()

    def join(d, carry):
        total, gate = carry
        theirs = bnd[d]
        higher = jnp.where(d > me, 1.0, 0.0)
        lower = jnp.where(d < me, 1.0, 0.0)
        same = jnp.where(theirs[:, id_lane : id_lane + 1] == ids_mine, 1.0, 0.0)
        mask = same * jnp.where(col_row < upper, higher, lower)
        return total + mask * theirs, jnp.maximum(gate, mask)

    total, gate = lax.fori_loop(
        0, n_series, join, (jnp.zeros((8, steps * wide), F32), jnp.zeros((8, 1), F32))
    )
    total = jnp.where(lane_p == id_lane, 0.0, total)
    z[...] = z[...] + exact(total, put, TN)
    owned = 1.0 - jnp.sum(put * jnp.where(col_row < upper, gate, 0.0), axis=0, keepdims=True)

    slot1 = lax.broadcasted_iota(jnp.int32, (1, slots), 1)
    level_of = jnp.zeros((1, slots), jnp.int32)
    for u in range(1, upper):
        level_of = jnp.where(slot1 >= offsets[u], u, level_of)
    tail = slots - 128
    node_weights = []
    for t in range(steps):
        full = z[t * wide : (t + 1) * wide, :]
        var = full[rank + t : rank + t + 1]
        weights = 1.0 / jnp.where(var > 0.0, var, 1.0)
        node_weights.append(weights)
        scaled = full * (weights * owned)
        right = split(full)
        send_matrix(steps + t, dot3(split(jnp.where(level_of == 0, scaled, 0.0)), right, NT))
        end = (right[0][:, tail:], right[1][:, tail:])
        for u in range(1, upper):
            left = jnp.where(level_of[:, tail:] == u, scaled[:, tail:], 0.0)
            send_matrix((u + 1) * steps + t, dot3(split(left), end, NT))

    def inv_copy(k):
        return pltpu.make_async_remote_copy(
            src_ref=invs.at[me], dst_ref=invs.at[me], send_sem=isem_s, recv_sem=isem_r,
            device_id={"series": lax.rem(me + k, n_series)}, device_id_type=MESH,
        )

    def solve():
        pltpu.make_async_copy(
            crecv.at[pl.ds(0, n_series - 1)], crecv.at[pl.ds(0, n_series - 1)], csem_r
        ).wait()
        shape = (rank, rank)
        eye = jnp.where(
            lax.broadcasted_iota(jnp.int32, shape, 0) == lax.broadcasted_iota(jnp.int32, shape, 1), 1.0, 0.0
        )
        a, below = unpack(lax.fori_loop(1, n_series, lambda d, c: c + crecv[d], crecv[0]))
        a = invert(a + eye, rank)
        invs[me] = pack(jnp.concatenate([a, exact(below[:, :rank], a, NN)], axis=0), rank)

        def start(k, c):
            inv_copy(k).start()
            return c

        lax.fori_loop(1, n_series, start, 0)
        pltpu.make_async_copy(
            invs.at[pl.ds(0, mats - 1)], invs.at[pl.ds(0, mats - 1)], isem_r
        ).wait()

    if n_series == mats:
        solve()
    else:
        pl.when(me < mats)(solve)

        @pl.when(me >= mats)
        def _():
            pltpu.make_async_copy(invs, invs, isem_r).wait()

    inverses, coefs = [], []
    for m in range(mats):
        matrix, below = unpack(invs[m])
        inverses.append(split(matrix))
        c = steps + m % steps
        coefs.append(below.T[:rank, c : c + 1])

    g[...] = jnp.zeros_like(g)
    for t in range(steps):
        full = z[t * wide : (t + 1) * wide, :]
        vec = full[:rank]
        weights = node_weights[t]
        res = full[rank + steps + t : rank + steps + t + 1]
        parts = split(vec)
        end = (parts[0][:, tail:], parts[1][:, tail:])
        solved = dot3(inverses[steps + t], parts, NN)
        solved_end = solved[:, tail:]
        coef = jnp.broadcast_to(coefs[steps + t], (rank, slots))
        scale = jnp.broadcast_to(weight_ref[t : t + 1, 1:2], (1, slots))
        for u in range(1, upper):
            m = (u + 1) * steps + t
            here = level_of[:, tail:] == u
            solved_end = jnp.where(here, dot3(inverses[m], end, NN), solved_end)
            coef = jnp.where(level_of == u, coefs[m], coef)
            scale = jnp.where(level_of == u, weight_ref[t : t + 1, u + 1 : u + 2], scale)
        solved = jnp.concatenate([solved[:, :tail], solved_end], axis=1)
        fitted = jnp.sum(vec * coef, axis=0, keepdims=True)
        white = weights * (res - fitted)
        leverage = jnp.sum(vec * solved, axis=0, keepdims=True)
        base = steps * rank
        g[t * rank : (t + 1) * rank, :] = scale * (solved * weights - coef * white)
        g[base + t : base + t + 1, :] = -scale * white
        g[base + steps + t : base + steps + t + 1, :] = (
            scale * 0.5 * (weights - weights * weights * leverage - white * white)
        )
    ghi, glo = split(g[...])
    height = g.shape[0]
    gs[:height, :] = ghi
    gs[height:, :] = glo

    pairs = n_tm // 2
    pair, side = mt // 2, lax.rem(mt, 2)
    sibling = pair * 2 + 1 - side

    def columns(j):
        cols = pl.ds(pl.multiple_of(j * part, part), part)
        both = bdot(gs[...], hot[:, cols], NN)
        up = both[:height] + both[height:]
        loading_sum = None
        for t in range(steps):
            vec = v[t * wide : t * wide + rank, cols]
            var = v[rank + t : rank + t + 1, cols]
            res = v[rank + steps + t : rank + steps + t + 1, cols]
            weights = 1.0 / var
            coef = coefs[t]
            scale = weight_ref[t : t + 1, 0:1]
            solved = dot3(inverses[t], split(vec), NN)
            fitted = jnp.sum(vec * coef, axis=0, keepdims=True)
            white = weights * (res - fitted)
            leverage = jnp.sum(vec * solved, axis=0, keepdims=True)
            base = steps * rank
            drift = up[t * rank : (t + 1) * rank] + scale * (solved * weights - coef * white)
            gdrift_ref[t, :, cols] = drift
            gloc_ref[t : t + 1, cols] = up[base + t : base + t + 1] - scale * white
            gvar_ref[t : t + 1, cols] = up[base + steps + t : base + steps + t + 1] + scale * 0.5 * (
                weights - weights * weights * leverage - white * white
            )
            loading_sum = drift if loading_sum is None else loading_sum + drift
        return loading_sum

    def send(slot, value, to):
        lsend[slot] = value
        copy = pltpu.make_async_remote_copy(
            src_ref=lsend.at[slot], dst_ref=lrecv.at[slot],
            send_sem=gsem_s.at[slot], recv_sem=gsem_r.at[slot],
            device_id={"tm": to}, device_id_type=MESH,
        )
        copy.start()
        return copy

    copies = []
    for q in range(1, pairs):
        there = lax.rem(pair + q, pairs) * 2
        near = send(2 * q - 2, columns(there + 1 - side), sibling)
        both_sum = columns(there + side)
        near.wait_recv()
        copies += [near, send(2 * q - 1, both_sum + lrecv[2 * q - 2], there + side)]
    near = send(2 * pairs - 2, columns(sibling), sibling)
    loading_sum = columns(mt)
    near.wait_recv()
    loading_sum = loading_sum + lrecv[2 * pairs - 2]
    for q in range(1, pairs):
        copies[2 * q - 1].wait_recv()
        loading_sum = loading_sum + lrecv[2 * q - 1]
    copies.append(near)
    gload_ref[...] = loading_sum

    for copy in loads + copies:
        copy.wait_send()
    pltpu.make_async_copy(
        bnd.at[pl.ds(0, n_series - 1)], bnd.at[pl.ds(0, n_series - 1)], bsem_s
    ).wait()

    def sent(own):
        held = cs.at[pl.ds(0, mats - 1 if own else mats)]
        pltpu.make_async_copy(held, held, csem_s).wait()
        if own:
            pltpu.make_async_copy(
                crecv.at[pl.ds(0, n_series - 1)], crecv.at[pl.ds(0, n_series - 1)], isem_s
            ).wait()

    if n_series == mats:
        sent(True)
    else:
        pl.when(me < mats)(functools.partial(sent, True))
        pl.when(me >= mats)(functools.partial(sent, False))


def local(target, location, variance, factor_drift, loading, node_ids, level_weight):
    steps, rank, count = factor_drift.shape
    upper = node_ids.shape[0]
    n_series, n_tm = lax.axis_size("series"), lax.axis_size("tm")
    slots = count // 4
    part = count // n_tm
    wide = rank + 16
    mats = (upper + 1) * steps
    height = steps * rank + 16
    vmem = pl.BlockSpec(memory_space=pltpu.VMEM)
    dma = pltpu.SemaphoreType.DMA
    operands = (target, location, variance, factor_drift, loading, node_ids, level_weight.T)
    operands = [pltpu.with_memory_space_constraint(a, pltpu.HBM) for a in operands]
    return pl.pallas_call(
        functools.partial(kernel, n_series, n_tm),
        out_shape=(
            jax.ShapeDtypeStruct((steps, count), F32),
            jax.ShapeDtypeStruct((steps, count), F32),
            jax.ShapeDtypeStruct((steps, rank, count), F32),
            jax.ShapeDtypeStruct((rank, part), F32),
        ),
        in_specs=[pl.BlockSpec(memory_space=pltpu.HBM)] * 7,
        out_specs=(vmem,) * 4,
        scratch_shapes=[
            pltpu.VMEM((steps, count), F32),
            pltpu.VMEM((steps, count), F32),
            pltpu.VMEM((steps, count), F32),
            pltpu.VMEM((steps, rank, count), BF16),
            pltpu.VMEM((rank, part), BF16),
            pltpu.VMEM((upper, count), jnp.int32),
            pltpu.VMEM((steps, upper + 1), F32),
            dma((7,)),
            pltpu.VMEM((n_tm, rank, part), BF16),
            pltpu.VMEM(((steps + 1) * rank + 32, count), BF16),
            pltpu.VMEM((slots, count), BF16),
            pltpu.VMEM((steps * wide, count), F32),
            pltpu.VMEM((steps * wide, slots), F32),
            pltpu.VMEM((n_series, 8, steps * wide), F32),
            pltpu.VMEM((mats, rank // 2 + 8, 2 * rank), F32),
            pltpu.VMEM((n_series, rank // 2 + 8, 2 * rank), F32),
            pltpu.VMEM((mats, rank // 2 + 8, 2 * rank), F32),
            pltpu.VMEM((height, slots), F32),
            pltpu.VMEM((2 * height, slots), BF16),
            pltpu.VMEM((n_tm, rank, part), F32),
            pltpu.VMEM((n_tm, rank, part), F32),
            dma((n_tm,)), dma((n_tm,)),
            dma, dma, dma, dma, dma, dma,
            dma((n_tm,)), dma((n_tm,)),
        ],
        compiler_params=pltpu.CompilerParams(
            collective_id=0, has_side_effects=True, vmem_limit_bytes=48 * 1024 * 1024
        ),
    )(*operands)


def solution(mesh):
    return jax.shard_map(
        local,
        mesh=mesh,
        in_specs=(
            P("tm", "series"),
            P("tm", "series"),
            P("tm", "series"),
            P("tm", None, "series"),
            P(None, ("series", "tm")),
            P(None, "series"),
            P(None, "tm"),
        ),
        out_specs=(
            P("tm", "series"),
            P("tm", "series"),
            P("tm", None, "series"),
            P(None, ("series", "tm")),
        ),
        check_vma=False,
    )
```

```python
import functools

import jax
import jax.numpy as jnp
from jax import lax
from jax.experimental import pallas as pl
from jax.experimental.pallas import tpu as pltpu
from jax.sharding import PartitionSpec as P

MESH = pl.DeviceIdType.MESH
F32 = jnp.float32
BF16 = jnp.bfloat16
SMALL = 16
NT = (((1,), (1,)), ((), ()))
NN = (((1,), (0,)), ((), ()))
TN = (((0,), (0,)), ((), ()))


def split(x):
    hi = x.astype(BF16)
    return hi, (x - hi.astype(F32)).astype(BF16)


def bdot(a, b, dims):
    return lax.dot_general(a, b, dims, preferred_element_type=F32)


def dot3(a, b, dims):
    ah, al = a
    bh, bl = b
    return bdot(ah, bh, dims) + (bdot(ah, bl, dims) + bdot(al, bh, dims))


def exact(a, b, dims):
    return lax.dot_general(
        a, b, dims, precision=lax.Precision.HIGHEST, preferred_element_type=F32
    )


def pack(value, rank):
    half = rank // 2
    left = jnp.concatenate([value[:half, :rank], value[rank : rank + 8, :rank]], axis=0)
    right = jnp.concatenate([value[half:rank, :rank], jnp.zeros((8, rank), F32)], axis=0)
    return jnp.concatenate([left, right], axis=1)


def unpack(packed):
    half, rank = packed.shape[0] - 8, packed.shape[1] // 2
    matrix = jnp.concatenate([packed[:half, :rank], packed[:half, rank:]], axis=0)
    return matrix, packed[half:]


def invert(a, size):
    lane = lax.broadcasted_iota(jnp.int32, a.shape, 1)
    row = lax.broadcasted_iota(jnp.int32, a.shape, 0)
    for k in range(size):
        pivot = 1.0 / a[k : k + 1, k : k + 1]
        col = a[:, k : k + 1]
        here = lane[:1] == k
        new_row = jnp.where(here, 1.0, a[k : k + 1, :]) * pivot
        rest = jnp.where(lane == k, 0.0, a) - col * new_row
        a = jnp.where(row == k, new_row, rest)
    return a


def kernel(
    n_series, n_tm,
    target_hbm, location_hbm, variance_hbm, drift_hbm, loading_hbm, ids_hbm, weight_hbm,
    gloc_ref, gvar_ref, gdrift_ref, gload_ref,
    target_ref, location_ref, variance_ref, drift_ref, loading_ref, ids_ref, weight_ref, in_sem,
    lbuf, x, hot, v, z, bnd, cs, crecv, invs, g, gs, lsend, lrecv,
    lsem_s, lsem_r, bsem_s, bsem_r, csem_s, csem_r, isem_s, isem_r, gsem_s, gsem_r,
):
    steps, rank, count = drift_hbm.shape
    upper = ids_hbm.shape[0]
    slots = hot.shape[0]
    wide = rank + 16
    mats = (upper + 1) * steps
    offsets = [0] + [slots - SMALL * (upper - 1 - i) for i in range(upper - 1)]
    part = count // n_tm
    me = lax.axis_index("series")
    mt = lax.axis_index("tm")

    barrier = pltpu.get_barrier_semaphore()
    ins = [
        pltpu.make_async_copy(src, dst, in_sem.at[i])
        for i, (src, dst) in enumerate((
            (loading_hbm, loading_ref), (ids_hbm, ids_ref), (target_hbm, target_ref),
            (location_hbm, location_ref), (variance_hbm, variance_ref),
            (drift_hbm, drift_ref), (weight_hbm, weight_ref),
        ))
    ]
    for copy in ins:
        copy.start()

    def hello(k, c):
        pl.semaphore_signal(
            barrier, inc=1, device_id={"series": lax.rem(me + k, n_series)}, device_id_type=MESH
        )
        return c

    lax.fori_loop(1, n_series, hello, 0)
    for k in range(1, n_tm):
        pl.semaphore_signal(
            barrier, inc=1, device_id={"tm": lax.rem(mt + k, n_tm)}, device_id_type=MESH
        )
    pl.semaphore_wait(barrier, n_series - 1 + n_tm - 1)

    loads = []
    ins[0].wait()
    for k in range(1, n_tm):
        loads.append(
            pltpu.make_async_remote_copy(
                src_ref=loading_ref, dst_ref=lbuf.at[mt],
                send_sem=lsem_s.at[k], recv_sem=lsem_r.at[k],
                device_id={"tm": lax.rem(mt + k, n_tm)}, device_id_type=MESH,
            )
        )
        loads[-1].start()
    lbuf[mt] = loading_ref[...]

    ins[1].wait()
    for u in range(upper):
        size = (offsets[1] if upper > 1 else slots) if u == 0 else SMALL
        member = ids_ref[u : u + 1, :] - ids_ref[u : u + 1, 0:1]
        for at in range(0, size, SMALL * 2 if size % (SMALL * 2) == 0 else SMALL):
            rows = min(SMALL * 2, size)
            slot = lax.broadcasted_iota(jnp.int32, (rows, count), 0) + at
            hot[offsets[u] + at : offsets[u] + at + rows, :] = jnp.where(
                slot == member, 1.0, 0.0
            ).astype(BF16)

    for copy in ins[2:]:
        copy.wait()
    residual = target_ref[...] - location_ref[...]
    variance = variance_ref[...]
    for t in range(steps):
        base = t * wide + rank
        v[base : base + 16, :] = jnp.zeros((16, count), F32)
        v[base : base + steps, :] = variance
        v[base + steps : base + 2 * steps, :] = residual
    aux = v[rank : rank + 8, :]
    one = aux.astype(BF16).astype(F32)
    two = (aux - one).astype(BF16).astype(F32)
    three = aux - one - two
    head = (steps + 1) * rank
    x[head : head + 32, :] = jnp.concatenate([one, two, three, jnp.zeros_like(one)], axis=0).astype(BF16)
    for t in range(steps):
        x[t * rank : (t + 1) * rank, :] = drift_ref[t]

    for copy in loads:
        copy.wait_recv()
    for j in range(n_tm):
        x[steps * rank : head, j * part : (j + 1) * part] = lbuf[j]
    loading = x[steps * rank : head, :].astype(F32)
    for t in range(steps):
        v[t * wide : t * wide + rank, :] = loading + drift_ref[t].astype(F32)

    sums = bdot(x[...], hot[...], NT)
    for t in range(steps):
        z[t * wide : t * wide + rank, :] = sums[t * rank : (t + 1) * rank] + sums[steps * rank : head]
        base = t * wide + rank
        z[base : base + 8, :] = (
            sums[head : head + 8] + sums[head + 8 : head + 16] + sums[head + 16 : head + 24]
        )
        z[base + 8 : base + 16, :] = jnp.zeros((8, slots), F32)

    row8 = lax.broadcasted_iota(jnp.int32, (8, slots), 0)
    slot8 = lax.broadcasted_iota(jnp.int32, (8, slots), 1)
    pick = jnp.zeros((8, slots), F32)
    put = jnp.zeros((8, slots), F32)
    col_row = lax.broadcasted_iota(jnp.int32, (8, 1), 0)
    ids_sent = jnp.full((8, 1), -1.0, F32)
    ids_mine = jnp.full((8, 1), -2.0, F32)
    for u in range(upper):
        first = ids_ref[u : u + 1, 0:1]
        last = ids_ref[u : u + 1, count - 1 : count]
        final = last - first + offsets[u]
        at_first = jnp.where(slot8 == offsets[u], 1.0, 0.0)
        at_last = jnp.where(slot8 == final, 1.0, 0.0)
        pick = jnp.where(row8 == u, at_first, jnp.where(row8 == u + upper, at_last, pick))
        put = jnp.where(row8 == u, at_last, jnp.where(row8 == u + upper, at_first, put))
        first = first.astype(F32)
        last = last.astype(F32)
        ids_sent = jnp.where(col_row == u, first, jnp.where(col_row == u + upper, last, ids_sent))
        ids_mine = jnp.where(col_row == u, last, jnp.where(col_row == u + upper, first, ids_mine))
    lane_p = lax.broadcasted_iota(jnp.int32, (8, steps * wide), 1)
    id_lane = rank + 8
    bnd[me] = jnp.where(lane_p == id_lane, ids_sent, exact(pick, z[...], NT))

    def bnd_copy(k):
        return pltpu.make_async_remote_copy(
            src_ref=bnd.at[me], dst_ref=bnd.at[me], send_sem=bsem_s, recv_sem=bsem_r,
            device_id={"series": lax.rem(me + k, n_series)}, device_id_type=MESH,
        )

    def bnd_start(k, c):
        bnd_copy(k).start()
        return c

    lax.fori_loop(1, n_series, bnd_start, 0)

    def send_matrix(m, whole):
        value = pack(whole, rank)

        @pl.when(me == m)
        def _():
            crecv[me] = value

        @pl.when(me != m)
        def _():
            cs[m] = value
            pltpu.make_async_remote_copy(
                src_ref=cs.at[m], dst_ref=crecv.at[me], send_sem=csem_s, recv_sem=csem_r,
                device_id={"series": jnp.int32(m)}, device_id_type=MESH,
            ).start()

    for t in range(steps):
        full = v[t * wide : (t + 1) * wide, :]
        weights = 1.0 / variance[t : t + 1]
        send_matrix(t, dot3(split(full * weights), split(full), NT))

    many = pltpu.make_async_copy(
        bnd.at[pl.ds(0, n_series - 1)], bnd.at[pl.ds(0, n_series - 1)], bsem_r
    )
    many.wait()

    def join(d, carry):
        total, gate = carry
        theirs = bnd[d]
        higher = jnp.where(d > me, 1.0, 0.0)
        lower = jnp.where(d < me, 1.0, 0.0)
        same = jnp.where(theirs[:, id_lane : id_lane + 1] == ids_mine, 1.0, 0.0)
        mask = same * jnp.where(col_row < upper, higher, lower)
        return total + mask * theirs, jnp.maximum(gate, mask)

    total, gate = lax.fori_loop(
        0, n_series, join, (jnp.zeros((8, steps * wide), F32), jnp.zeros((8, 1), F32))
    )
    total = jnp.where(lane_p == id_lane, 0.0, total)
    z[...] = z[...] + exact(total, put, TN)
    owned = 1.0 - jnp.sum(put * jnp.where(col_row < upper, gate, 0.0), axis=0, keepdims=True)

    slot1 = lax.broadcasted_iota(jnp.int32, (1, slots), 1)
    level_of = jnp.zeros((1, slots), jnp.int32)
    for u in range(1, upper):
        level_of = jnp.where(slot1 >= offsets[u], u, level_of)
    tail = slots - 128
    node_weights = []
    for t in range(steps):
        full = z[t * wide : (t + 1) * wide, :]
        var = full[rank + t : rank + t + 1]
        weights = 1.0 / jnp.where(var > 0.0, var, 1.0)
        node_weights.append(weights)
        scaled = full * (weights * owned)
        right = split(full)
        cs[steps + t] = pack(dot3(split(jnp.where(level_of == 0, scaled, 0.0)), right, NT), rank)
        end = (right[0][:, tail:], right[1][:, tail:])
        for u in range(1, upper):
            left = jnp.where(level_of[:, tail:] == u, scaled[:, tail:], 0.0)
            cs[(u + 1) * steps + t] = pack(dot3(split(left), end, NT), rank)

    for k in range(1, mats - steps + 1):
        m = steps + lax.rem(me + k, mats - steps)

        @pl.when(me == m)
        def _():
            crecv[me] = cs[m]

        @pl.when(me != m)
        def _():
            pltpu.make_async_remote_copy(
                src_ref=cs.at[m], dst_ref=crecv.at[me], send_sem=csem_s, recv_sem=csem_r,
                device_id={"series": m}, device_id_type=MESH,
            ).start()

    def inv_copy(k):
        return pltpu.make_async_remote_copy(
            src_ref=invs.at[me], dst_ref=invs.at[me], send_sem=isem_s, recv_sem=isem_r,
            device_id={"series": lax.rem(me + k, n_series)}, device_id_type=MESH,
        )

    def solve():
        pltpu.make_async_copy(
            crecv.at[pl.ds(0, n_series - 1)], crecv.at[pl.ds(0, n_series - 1)], csem_r
        ).wait()
        shape = (rank, rank)
        eye = jnp.where(
            lax.broadcasted_iota(jnp.int32, shape, 0) == lax.broadcasted_iota(jnp.int32, shape, 1), 1.0, 0.0
        )
        a, below = unpack(lax.fori_loop(1, n_series, lambda d, c: c + crecv[d], crecv[0]))
        a = invert(a + eye, rank)
        invs[me] = pack(jnp.concatenate([a, exact(below[:, :rank], a, NN)], axis=0), rank)

        def start(k, c):
            inv_copy(k).start()
            return c

        lax.fori_loop(1, n_series, start, 0)
        pltpu.make_async_copy(
            invs.at[pl.ds(0, mats - 1)], invs.at[pl.ds(0, mats - 1)], isem_r
        ).wait()

    if n_series == mats:
        solve()
    else:
        pl.when(me < mats)(solve)

        @pl.when(me >= mats)
        def _():
            pltpu.make_async_copy(invs, invs, isem_r).wait()

    inverses, coefs = [], []
    for m in range(mats):
        matrix, below = unpack(invs[m])
        inverses.append(split(matrix))
        c = steps + m % steps
        coefs.append(below.T[:rank, c : c + 1])

    g[...] = jnp.zeros_like(g)
    for t in range(steps):
        full = z[t * wide : (t + 1) * wide, :]
        vec = full[:rank]
        weights = node_weights[t]
        res = full[rank + steps + t : rank + steps + t + 1]
        parts = split(vec)
        end = (parts[0][:, tail:], parts[1][:, tail:])
        solved = dot3(inverses[steps + t], parts, NN)
        solved_end = solved[:, tail:]
        coef = jnp.broadcast_to(coefs[steps + t], (rank, slots))
        scale = jnp.broadcast_to(weight_ref[t : t + 1, 1:2], (1, slots))
        for u in range(1, upper):
            m = (u + 1) * steps + t
            here = level_of[:, tail:] == u
            solved_end = jnp.where(here, dot3(inverses[m], end, NN), solved_end)
            coef = jnp.where(level_of == u, coefs[m], coef)
            scale = jnp.where(level_of == u, weight_ref[t : t + 1, u + 1 : u + 2], scale)
        solved = jnp.concatenate([solved[:, :tail], solved_end], axis=1)
        fitted = jnp.sum(vec * coef, axis=0, keepdims=True)
        white = weights * (res - fitted)
        leverage = jnp.sum(vec * solved, axis=0, keepdims=True)
        base = steps * rank
        g[t * rank : (t + 1) * rank, :] = scale * (solved * weights - coef * white)
        g[base + t : base + t + 1, :] = -scale * white
        g[base + steps + t : base + steps + t + 1, :] = (
            scale * 0.5 * (weights - weights * weights * leverage - white * white)
        )
    ghi, glo = split(g[...])
    height = g.shape[0]
    gs[:height, :] = ghi
    gs[height:, :] = glo

    copies = []
    for k in list(range(1, n_tm)) + [0]:
        j = lax.rem(mt + k, n_tm)
        cols = pl.ds(pl.multiple_of(j * part, part), part)
        both = bdot(gs[...], hot[:, cols], NN)
        up = both[:height] + both[height:]
        loading_sum = None
        for t in range(steps):
            vec = v[t * wide : t * wide + rank, cols]
            var = v[rank + t : rank + t + 1, cols]
            res = v[rank + steps + t : rank + steps + t + 1, cols]
            weights = 1.0 / var
            coef = coefs[t]
            scale = weight_ref[t : t + 1, 0:1]
            solved = dot3(inverses[t], split(vec), NN)
            fitted = jnp.sum(vec * coef, axis=0, keepdims=True)
            white = weights * (res - fitted)
            leverage = jnp.sum(vec * solved, axis=0, keepdims=True)
            base = steps * rank
            drift = up[t * rank : (t + 1) * rank] + scale * (solved * weights - coef * white)
            gdrift_ref[t, :, cols] = drift
            gloc_ref[t : t + 1, cols] = up[base + t : base + t + 1] - scale * white
            gvar_ref[t : t + 1, cols] = up[base + steps + t : base + steps + t + 1] + scale * 0.5 * (
                weights - weights * weights * leverage - white * white
            )
            loading_sum = drift if loading_sum is None else loading_sum + drift
        if k:
            lsend[k] = loading_sum
            copy = pltpu.make_async_remote_copy(
                src_ref=lsend.at[k], dst_ref=lrecv.at[k],
                send_sem=gsem_s.at[k], recv_sem=gsem_r.at[k],
                device_id={"tm": j}, device_id_type=MESH,
            )
            copy.start()
            copies.append(copy)
    for k, copy in zip(range(1, n_tm), copies):
        copy.wait_recv()
        loading_sum = loading_sum + lrecv[k]
    gload_ref[...] = loading_sum

    for copy in loads + copies:
        copy.wait_send()
    pltpu.make_async_copy(
        bnd.at[pl.ds(0, n_series - 1)], bnd.at[pl.ds(0, n_series - 1)], bsem_s
    ).wait()

    def sent(own):
        held = cs.at[pl.ds(0, mats - 1 if own else mats)]
        pltpu.make_async_copy(held, held, csem_s).wait()
        if own:
            pltpu.make_async_copy(
                crecv.at[pl.ds(0, n_series - 1)], crecv.at[pl.ds(0, n_series - 1)], isem_s
            ).wait()

    if n_series == mats:
        sent(True)
    else:
        pl.when(me < mats)(functools.partial(sent, True))
        pl.when(me >= mats)(functools.partial(sent, False))


def local(target, location, variance, factor_drift, loading, node_ids, level_weight):
    steps, rank, count = factor_drift.shape
    upper = node_ids.shape[0]
    n_series, n_tm = lax.axis_size("series"), lax.axis_size("tm")
    slots = count // 4
    part = count // n_tm
    wide = rank + 16
    mats = (upper + 1) * steps
    height = steps * rank + 16
    vmem = pl.BlockSpec(memory_space=pltpu.VMEM)
    dma = pltpu.SemaphoreType.DMA
    operands = (target, location, variance, factor_drift, loading, node_ids, level_weight.T)
    operands = [pltpu.with_memory_space_constraint(a, pltpu.HBM) for a in operands]
    return pl.pallas_call(
        functools.partial(kernel, n_series, n_tm),
        out_shape=(
            jax.ShapeDtypeStruct((steps, count), F32),
            jax.ShapeDtypeStruct((steps, count), F32),
            jax.ShapeDtypeStruct((steps, rank, count), F32),
            jax.ShapeDtypeStruct((rank, part), F32),
        ),
        in_specs=[pl.BlockSpec(memory_space=pltpu.HBM)] * 7,
        out_specs=(vmem,) * 4,
        scratch_shapes=[
            pltpu.VMEM((steps, count), F32),
            pltpu.VMEM((steps, count), F32),
            pltpu.VMEM((steps, count), F32),
            pltpu.VMEM((steps, rank, count), BF16),
            pltpu.VMEM((rank, part), BF16),
            pltpu.VMEM((upper, count), jnp.int32),
            pltpu.VMEM((steps, upper + 1), F32),
            dma((7,)),
            pltpu.VMEM((n_tm, rank, part), BF16),
            pltpu.VMEM(((steps + 1) * rank + 32, count), BF16),
            pltpu.VMEM((slots, count), BF16),
            pltpu.VMEM((steps * wide, count), F32),
            pltpu.VMEM((steps * wide, slots), F32),
            pltpu.VMEM((n_series, 8, steps * wide), F32),
            pltpu.VMEM((mats, rank // 2 + 8, 2 * rank), F32),
            pltpu.VMEM((n_series, rank // 2 + 8, 2 * rank), F32),
            pltpu.VMEM((mats, rank // 2 + 8, 2 * rank), F32),
            pltpu.VMEM((height, slots), F32),
            pltpu.VMEM((2 * height, slots), BF16),
            pltpu.VMEM((n_tm, rank, part), F32),
            pltpu.VMEM((n_tm, rank, part), F32),
            dma((n_tm,)), dma((n_tm,)),
            dma, dma, dma, dma, dma, dma,
            dma((n_tm,)), dma((n_tm,)),
        ],
        compiler_params=pltpu.CompilerParams(
            collective_id=0, has_side_effects=True, vmem_limit_bytes=48 * 1024 * 1024
        ),
    )(*operands)


def solution(mesh):
    return jax.shard_map(
        local,
        mesh=mesh,
        in_specs=(
            P("tm", "series"),
            P("tm", "series"),
            P("tm", "series"),
            P("tm", None, "series"),
            P(None, ("series", "tm")),
            P(None, "series"),
            P(None, "tm"),
        ),
        out_specs=(
            P("tm", "series"),
            P("tm", "series"),
            P("tm", None, "series"),
            P(None, ("series", "tm")),
        ),
        check_vma=False,
    )
```
